128 devices in a mesh: row: 16 (over x, y), col: 8 (over z, core).
Axes of the slice: x: 4, y: 4, z: 4, core: 2. Of those that a mesh axis runs over, the one named last changes fastest.
Arguments:
- tile_values: float32 [40960, 128, 128], P(('row', 'col')), may hold values from 0 to 67108.87
- tile_rows: int32 [40960], P(('row', 'col')), may hold values from 0 to 127
- tile_cols: int32 [40960], P(('row', 'col')), may hold values from 0 to 255
- tile_patterns: int32 [40960], P(('row', 'col')), may hold values from 0 to 65535
- tile_counts: int32 [128], P(('row', 'col')), may hold values from 80 to 320, as said below
- factor: float32 [262144, 64], P(('row', 'col')), may hold values from 0.05 to 10, as said below
Outputs:
- factor_next: float32 [262144, 64], P(('row', 'col'))
The draws below stay inside these ranges and needn't reach their ends.
Inputs may be any that keep to these rules, and one draw needn't show every extreme that they name: `tile_counts`: every device has at least a quarter of its slots live, and some device has all 320 live. `factor`: entries are positive.
All inputs are finite; a program needn't handle non-finite values.
Results may differ from the reference program's by a relative error of at most 0.0003.
Values sent between devices are 32-bit elements; how exact they have to be, the bound alone decides.
No kernel may reach another device: no remote copies, remote signals or barrier semaphores. Data moves between devices by JAX's collectives and lax.ppermute only.
A program may use at most 192 MiB of HBM per device.

```python
import jax
import jax.numpy as jnp
from jax import lax

RANK = 64
TILE = 128
SLOTS = 320
ITEMS = 262144
TILE_ROWS = 128
TILE_COLS = 256
ALL_SLOTS = 40960
N_COL = 8
DEVICES = 128


def draw_tile_counts(key, part):
    key = jax.random.fold_in(key, 11)
    first, second = jax.random.split(key)
    counts = jax.random.randint(first, (DEVICES,), max(1, SLOTS // 4), SLOTS + 1)
    chosen = jax.random.randint(second, (), 0, DEVICES)
    return jnp.where(jnp.arange(DEVICES) == chosen, SLOTS, counts).astype(jnp.int32)


def draw_factor(key, part):
    key = jax.random.fold_in(key, 7)
    first = jax.random.fold_in(key, 0)
    base = jax.random.uniform(first, (ITEMS, RANK), jnp.float32, 0.1, 1.0)
    scale = 1.0 + 2.0 * jnp.arange(ITEMS, dtype=jnp.float32)[:, None] / (ITEMS - 1)
    return (base * scale).astype(jnp.float32)


def plant(values, key, least, high):
    place = [jax.random.randint(jax.random.fold_in(key, axis), (), 0, length) for axis, length in enumerate(values.shape)]
    longest = values.shape.index(max(values.shape))
    next_to = place[:longest] + [(place[longest] + 1) % values.shape[longest]] + place[longest + 1:]
    return values.at[tuple(place)].set(least).at[tuple(next_to)].set(high)


def level_of(own_key, shape, shards, smallest, largest):
    gain, own = 1.0, jax.random.fold_in(own_key, 6)
    for position, parts in shards:
        heights = jnp.exp(jax.random.uniform(jax.random.fold_in(own, position), (parts,), jnp.float32, smallest / len(shards), largest / len(shards)))
        gain = gain * jnp.repeat(heights, shape[position] // parts).reshape([-1 if axis == position else 1 for axis in range(len(shape))])
    return gain


def setup_inputs(seed: int = 0) -> dict:
    streams_of = jax.random.split(jax.random.key(seed), 7)
    tile_values = jnp.clip(67108.87 * jax.random.uniform(streams_of[0], (ALL_SLOTS, TILE, TILE), jnp.float32) ** level_of(streams_of[0], (ALL_SLOTS, TILE, TILE), ((0, 128),), -0.2, 0.2), 0.0, 67108.87)
    tile_rows = plant(jax.random.randint(streams_of[1], (ALL_SLOTS,), 0, TILE_ROWS), jax.random.fold_in(streams_of[1], 1), 0, TILE_ROWS - 1).astype(jnp.int32)
    tile_cols = plant(jax.random.randint(streams_of[2], (ALL_SLOTS,), 0, TILE_COLS), jax.random.fold_in(streams_of[2], 1), 0, TILE_COLS - 1).astype(jnp.int32)
    tile_patterns = plant(jax.random.randint(streams_of[3], (ALL_SLOTS,), 0, 65536), jax.random.fold_in(streams_of[3], 1), 0, 65535).astype(jnp.int32)
    tile_counts = draw_tile_counts(jax.random.fold_in(streams_of[6], 71), 0)
    factor = draw_factor(jax.random.fold_in(streams_of[6], 71), 0)
    return dict(tile_values=tile_values, tile_rows=tile_rows, tile_cols=tile_cols, tile_patterns=tile_patterns, tile_counts=tile_counts, factor=factor)


def expand_pattern(patterns):
    shifts = jnp.arange(16, dtype=jnp.int32)
    bits = jnp.bitwise_and(jnp.right_shift(patterns[:, None], shifts[None, :]), 1)
    return bits.reshape(-1, 4, 4).astype(jnp.float32)


def masked_tiles(values, patterns):
    sub_mask = expand_pattern(patterns)
    count_tiles = values.shape[0]
    edge = values.shape[1] // 4
    shaped = values.reshape(count_tiles, 4, edge, 4, edge) * sub_mask[:, :, None, :, None]
    return shaped.reshape(count_tiles, values.shape[1], values.shape[2])


def hals_sweep(factor, image, gram_matrix):
    def update(column, current):
        gram_col = lax.dynamic_slice_in_dim(gram_matrix, column, 1, 1)
        fitted = jnp.dot(current, gram_col, precision=lax.Precision.HIGHEST)[:, 0]
        diagonal = lax.dynamic_index_in_dim(gram_col[:, 0], column, 0, False)
        target = lax.dynamic_index_in_dim(image, column, 1, False)
        old_col = lax.dynamic_index_in_dim(current, column, 1, False)
        fresh = jnp.maximum(old_col + (target - fitted) / diagonal, 0.0)
        return lax.dynamic_update_index_in_dim(current, fresh, column, 1)
    return lax.fori_loop(0, gram_matrix.shape[0], update, factor)


def reference(tile_values, tile_rows, tile_cols, tile_patterns, tile_counts, factor):
    factor_tiles = factor.reshape(ITEMS // TILE, TILE, RANK)
    values_dev = tile_values.reshape(DEVICES, SLOTS, TILE, TILE)
    rows_dev = tile_rows.reshape(DEVICES, SLOTS)
    cols_dev = tile_cols.reshape(DEVICES, SLOTS)
    patt_dev = tile_patterns.reshape(DEVICES, SLOTS)

    def device_step(accum_rows, device):
        row_index = device // N_COL
        col_index = device % N_COL
        values = lax.dynamic_index_in_dim(values_dev, device, 0, False)
        local_rows = lax.dynamic_index_in_dim(rows_dev, device, 0, False)
        local_cols = lax.dynamic_index_in_dim(cols_dev, device, 0, False)
        patterns = lax.dynamic_index_in_dim(patt_dev, device, 0, False)
        live_count = lax.dynamic_index_in_dim(tile_counts, device, 0, False)
        tiles_now = masked_tiles(values, patterns)
        global_cols = (col_index * TILE_COLS + local_cols).astype(jnp.int32)
        global_rows = (row_index * TILE_ROWS + local_rows).astype(jnp.int32)
        blocks = factor_tiles[global_cols]
        products = jnp.einsum("sij,sjk->sik", tiles_now.astype(jnp.float32), blocks.astype(jnp.float32), precision=lax.Precision.HIGHEST)
        live_slots = (jnp.arange(SLOTS, dtype=jnp.int32) < live_count).astype(jnp.float32)
        products = products * live_slots[:, None, None]
        return accum_rows.at[global_rows].add(products), None

    start = jnp.zeros((ITEMS // TILE, TILE, RANK), jnp.float32)
    accum_rows, unused = lax.scan(device_step, start, jnp.arange(DEVICES, dtype=jnp.int32))
    image = accum_rows.reshape(ITEMS, RANK)
    gram_matrix = jnp.dot(factor.T, factor, precision=lax.Precision.HIGHEST)
    return hals_sweep(factor, image, gram_matrix)
```

```python
import functools

import jax
import jax.numpy as jnp
from jax import lax
from jax.experimental import pallas as pl
from jax.experimental.pallas import tpu as pltpu
from jax.sharding import PartitionSpec as P

NX = NY = NZ = 4
AXES = ("row", "col")
RANK, TILE, SLOTS = 64, 128, 320
PAIRS = 1
WIDTH = RANK // PAIRS
GRAM_ROWS = RANK * RANK // TILE
HALF = 8
ITEM_TILES = 16
ROW_TILES = 128
DUMMY = ROW_TILES
UNROLL = 8
BATCH = 32
PLACE = (0, 2, 3, 1)

WHOLE = pl.BlockSpec(memory_space=pltpu.VMEM)
SCALARS = pl.BlockSpec(memory_space=pltpu.SMEM)


def params(mib):
    return pltpu.CompilerParams(vmem_limit_bytes=mib * 2**20)


def coords(d):
    return d // 32, (d // 8) % 4, (d // 2) % 4, d % 2


def number(x, y, z, core):
    return ((x * NY + y) * NZ + z) * 2 + core


def shift(array, axis, step):
    pairs = []
    for d in range(128):
        place = list(coords(d))
        place[axis] = (place[axis] + step) % (2 if axis == 3 else 4)
        pairs.append((d, number(*place)))
    return lax.ppermute(array, AXES, pairs)


def spread(array):
    pairs = []
    for d in range(128):
        x, y, z, core = coords(d)
        pairs.append((d, number((x + z) % 4, y if core == 0 else 3 - y, x, y // 2)))
    return lax.ppermute(array, AXES, pairs)


def ring(block, axis):
    half = block.shape[0] // 2
    below, above = shift(block, axis, 1), shift(block, axis, -1)
    far = jnp.concatenate([shift(below[:half], axis, 1), shift(above[half:], axis, -1)])
    return [block, below, above, far]


def first_kernel(factor_ref, *outs):
    gram = jnp.zeros((RANK, RANK), jnp.float32)
    for tile in range(ITEM_TILES):
        piece = factor_ref[:, tile * TILE : (tile + 1) * TILE]
        gram += lax.dot_general(
            piece, piece, (((1,), (1,)), ((), ())), precision=lax.Precision.HIGHEST, preferred_element_type=jnp.float32
        )
        side, place = tile // HALF, tile % HALF
        for pair in range(PAIRS):
            outs[2 * pair + side][place * WIDTH : (place + 1) * WIDTH, :] = piece[pair * WIDTH : (pair + 1) * WIDTH]
    outs[0][HALF * WIDTH :, :] = jnp.concatenate([gram[:GRAM_ROWS], gram[GRAM_ROWS:]], axis=1)


def first(factor):
    rows = HALF * WIDTH
    shapes = []
    for pair in range(PAIRS):
        shapes += [rows + (GRAM_ROWS if pair == 0 else 0), rows]
    return pl.pallas_call(
        first_kernel,
        in_specs=[WHOLE],
        out_specs=[WHOLE] * (2 * PAIRS),
        out_shape=[jax.ShapeDtypeStruct((n, TILE), jnp.float32) for n in shapes],
        compiler_params=params(8),
        name="first",
    )(factor)


def split(value):
    high = value.astype(jnp.bfloat16)
    return high, (value - high.astype(jnp.float32)).astype(jnp.bfloat16)


def prepare_kernel(count, patterns, values_ref, tiles_ref):
    step = pl.program_id(0)
    bit = 4 * (lax.broadcasted_iota(jnp.int32, (TILE, TILE), 0) // 32)
    bit += lax.broadcasted_iota(jnp.int32, (TILE, TILE), 1) // 32
    flag = jnp.left_shift(1, bit)

    @pl.when(step * BATCH < count[0])
    def _():
        for u in range(BATCH):
            slot = step * BATCH + u
            kept = jnp.where((patterns[slot] & flag) != 0, values_ref[u], 0.0)
            high, low = split(kept.T)
            tiles_ref[slot, :TILE, :] = high
            tiles_ref[slot, TILE:, :] = low


def prepare(count, patterns, values):
    return pl.pallas_call(
        prepare_kernel,
        grid_spec=pltpu.PrefetchScalarGridSpec(
            num_scalar_prefetch=2,
            grid=(SLOTS // BATCH,),
            in_specs=[
                pl.BlockSpec(
                    (BATCH, TILE, TILE), lambda i, count, pats: (jnp.minimum(i, (count[0] - 1) // BATCH), 0, 0)
                )
            ],
            out_specs=WHOLE,
        ),
        out_shape=pltpu.VMEM((SLOTS, 2 * TILE, TILE), jnp.bfloat16),
        compiler_params=params(30),
        name="prepare",
    )(count, patterns, values)


def plan(rows, cols, count):
    row, col = lax.axis_index("row"), lax.axis_index("col")
    x, y, z, core = row // NY, row % NY, col // 2, col % 2
    shard, tile = cols // ITEM_TILES, cols % ITEM_TILES
    from_z, from_core = (shard % 8) // 2, shard % 2
    from_y = 2 * core + shard // 8
    to_x = (z + from_z) % NX
    to_y = jnp.where(from_core == 0, from_y, 3 - from_y)
    place = jnp.array(PLACE, jnp.int32)

    def placed(d):
        return jnp.where(d == 0, 0, jnp.where(d == 1, 2, jnp.where(d == 2, 3, 1)))

    px, py = placed((to_x - x) % 4), placed((to_y - y) % 4)
    side = tile // HALF
    part = jnp.where(side == 0, py, px)
    block = jnp.where(side == 0, px, py)
    owner = rows // ITEM_TILES
    target = ((owner % 2 + core) % 2) * 64 + ((owner // 2 - z) % 4) * ITEM_TILES + rows % ITEM_TILES
    slots = jnp.arange(SLOTS, dtype=jnp.int32)
    packed = slots + target * 512 + block * 131072 + (tile % HALF) * 524288
    key = jnp.where(slots < count[0], part * 2 + side, 8)
    before = (key[None, :] < key[:, None]) | ((key[None, :] == key[:, None]) & (slots[None, :] < slots[:, None]))
    position = jnp.sum(before.astype(jnp.int32), axis=1)
    places = jnp.arange(SLOTS + 2 * UNROLL, dtype=jnp.int32)
    order = jnp.sum(jnp.where(position[None, :] == places[:, None], packed[None, :], 0), axis=1)
    starts = jnp.sum((key[None, :] < jnp.arange(9, dtype=jnp.int32)[:, None]).astype(jnp.int32), axis=1)
    return order, starts


def products(order, lower, upper, tiles_ref, panel_ref, stride, sums_ref):
    def body(group, carry):
        found = []
        for u in range(UNROLL):
            at = lower + group * UNROLL + u
            word = order[at]
            slot = word & 511
            target = jnp.where(at < upper, (word >> 9) & 255, DUMMY)
            start = ((word >> 17) & 3) * stride + ((word >> 19) & 7) * WIDTH
            high, low = split(panel_ref[pl.ds(pl.multiple_of(start, 8), WIDTH), :])
            both = jnp.concatenate([high, low], axis=0)
            result = jnp.dot(
                jnp.concatenate([both, both], axis=1), tiles_ref[slot], preferred_element_type=jnp.float32
            )
            found.append((target, result[:WIDTH] + result[WIDTH:]))
        for target, result in found:
            sums_ref[pl.ds(pl.multiple_of(target * WIDTH, 8), WIDTH), :] += result
        return carry

    lax.fori_loop(0, (upper - lower + UNROLL - 1) // UNROLL, body, 0)


def part_kernel(part, with_gram, order, starts, tiles_ref, a_ref, b_ref, old_ref, sums_ref):
    stride = a_ref.shape[0] // 4
    bottom = (ROW_TILES + 1) * WIDTH
    if part == 0:
        sums_ref[...] = jnp.zeros_like(sums_ref)
    if with_gram:
        for block in range(4):
            sums_ref[bottom:, :] += a_ref[block * stride + HALF * WIDTH : (block + 1) * stride, :]
    products(order, starts[2 * part], starts[2 * part + 1], tiles_ref, a_ref, stride, sums_ref)
    products(order, starts[2 * part + 1], starts[2 * part + 2], tiles_ref, b_ref, HALF * WIDTH, sums_ref)


def add_part(part, with_gram, order, starts, tiles, a, b, sums):
    rows = (ROW_TILES + 1) * WIDTH + (GRAM_ROWS if with_gram else 0)
    kernel = functools.partial(part_kernel, part, with_gram)
    operands = [order, starts, tiles, a, b]
    if part > 0:
        operands.append(sums)
    else:
        kernel = functools.partial(lambda k, *refs: k(*refs[:5], None, refs[5]), kernel)
    return pl.pallas_call(
        kernel,
        in_specs=[SCALARS] * 2 + [WHOLE] * (len(operands) - 2),
        out_specs=WHOLE,
        out_shape=pltpu.VMEM((rows, TILE), jnp.float32),
        input_output_aliases={5: 0} if part > 0 else {},
        compiler_params=params(6),
        name="part",
    )(*operands)


def deal_kernel(with_gram, sums_ref, core_ref):
    rows = 64 * WIDTH
    core_ref[:rows, :] = sums_ref[rows : 2 * rows, :]
    if with_gram:
        core_ref[rows:, :] = sums_ref[2 * rows + WIDTH :, :]


def deal(with_gram, sums):
    rows = 64 * WIDTH + (GRAM_ROWS if with_gram else 0)
    return pl.pallas_call(
        functools.partial(deal_kernel, with_gram),
        in_specs=[WHOLE],
        out_specs=WHOLE,
        out_shape=jax.ShapeDtypeStruct((rows, TILE), jnp.float32),
        compiler_params=params(12),
        name="deal",
    )(sums)


def joined_kernel(with_gram, sums_ref, other_ref, up_ref, down_ref, kept_ref):
    block = ITEM_TILES * WIDTH
    half = block // 2
    total = 4 * block

    def both(start, size):
        return sums_ref[start : start + size, :] + other_ref[start : start + size, :]

    up_ref[:half, :] = both(2 * block, half)
    down_ref[:half, :] = both(2 * block + half, half)
    for place, source in enumerate((0, 1, 3)):
        kept_ref[place * block : (place + 1) * block, :] = both(source * block, block)
    if with_gram:
        gram = sums_ref[2 * total + WIDTH :, :] + other_ref[total:, :]
        up_ref[half:, :] = gram
        down_ref[half:, :] = gram
        kept_ref[3 * block :, :] = gram


def joined(with_gram, sums, other):
    block = ITEM_TILES * WIDTH
    extra = GRAM_ROWS if with_gram else 0
    shapes = [block // 2 + extra, block // 2 + extra, 3 * block + extra]
    return pl.pallas_call(
        functools.partial(joined_kernel, with_gram),
        in_specs=[WHOLE] * 2,
        out_specs=[WHOLE] * 3,
        out_shape=[jax.ShapeDtypeStruct((n, TILE), jnp.float32) for n in shapes],
        compiler_params=params(16),
        name="joined",
    )(sums, other)


def onward_kernel(with_gram, kept_ref, below_ref, above_ref, up_ref, down_ref):
    block = ITEM_TILES * WIDTH
    half = block // 2
    up_ref[:half, :] = kept_ref[block : block + half, :] + below_ref[:half, :]
    up_ref[half:block, :] = kept_ref[block + half : 2 * block, :]
    down_ref[:half, :] = kept_ref[2 * block : 2 * block + half, :]
    down_ref[half:block, :] = kept_ref[2 * block + half : 3 * block, :] + above_ref[:half, :]
    if with_gram:
        up_ref[block:, :] = below_ref[half:, :]


def onward(with_gram, kept, below, above):
    block = ITEM_TILES * WIDTH
    extra = GRAM_ROWS if with_gram else 0
    return pl.pallas_call(
        functools.partial(onward_kernel, with_gram),
        in_specs=[WHOLE] * 3,
        out_specs=[WHOLE] * 2,
        out_shape=[jax.ShapeDtypeStruct((n, TILE), jnp.float32) for n in (block + extra, block)],
        compiler_params=params(12),
        name="onward",
    )(kept, below, above)


def scatter(with_gram, sums):
    other = shift(deal(with_gram, sums), 3, 1)
    up, down, kept = joined(with_gram, sums, other)
    below, above = shift(up, 2, 1), shift(down, 2, -1)
    up, down = onward(with_gram, kept, below, above)
    return kept, below, above, shift(up, 2, 1), shift(down, 2, -1)


def sweep_kernel(*refs):
    blocks = refs[: 7 * PAIRS]
    out_ref, resid, state, moves, gram_ref, inverse_ref, gram_s, inverse_s, sems = refs[7 * PAIRS :]
    block = ITEM_TILES * WIDTH
    kept, below, above, last = blocks[0], blocks[1], blocks[2], blocks[3]
    packed = (kept[3 * block :, :] + below[block // 2 :, :]) + (above[block // 2 :, :] + last[block:, :])
    gram_ref[...] = packed
    inverse_ref[...] = 1.0 / packed
    copies = [
        pltpu.make_async_copy(gram_ref, gram_s, sems.at[0]),
        pltpu.make_async_copy(inverse_ref, inverse_s, sems.at[1]),
    ]
    for copy in copies:
        copy.start()
    gram = jnp.concatenate([packed[:, :RANK], packed[:, RANK:]], axis=0)
    for tile in range(ITEM_TILES):
        side, place = tile // HALF, tile % HALF
        images, olds = [], []
        for pair in range(PAIRS):
            kept, _, _, up, down, a, b = blocks[7 * pair : 7 * pair + 7]
            rows = slice(tile * WIDTH, (tile + 1) * WIDTH)
            images.append(kept[rows, :] + (up[rows, :] + down[rows, :]))
            olds.append((a, b)[side][place * WIDTH : (place + 1) * WIDTH, :])
        image, old = jnp.concatenate(images, axis=0), jnp.concatenate(olds, axis=0)
        fitted = jnp.dot(gram, old, precision=lax.Precision.HIGHEST, preferred_element_type=jnp.float32)
        resid[tile * RANK : (tile + 1) * RANK, :] = image - fitted
        state[tile * RANK : (tile + 1) * RANK, :] = old
    for copy in copies:
        copy.wait()

    def entry(ref, j, k):
        return ref[j % GRAM_ROWS, (j // GRAM_ROWS) * RANK + k]

    def column(ref, k):
        return ref[pl.ds(k, ITEM_TILES, stride=RANK), :]

    for group in range(RANK // 8):
        columns = range(group * 8, group * 8 + 8)
        left = tuple(column(resid, k) for k in columns)
        if group:

            def earlier(k, left):
                move = moves[k]
                return tuple(r - move * entry(gram_s, j, k) for r, j in zip(left, columns))

            left = lax.fori_loop(0, group * 8, earlier, left, unroll=4)
        left = list(left)
        for i, k in enumerate(columns):
            old = column(state, k)
            fresh = jnp.maximum(old + left[i] * entry(inverse_s, k, k), 0.0)
            move = fresh - old
            moves[k] = move
            state[pl.ds(k, ITEM_TILES, stride=RANK), :] = fresh
            for m in range(i + 1, 8):
                left[m] = left[m] - move * entry(gram_s, columns[m], k)
    for tile in range(ITEM_TILES):
        out_ref[:, tile * TILE : (tile + 1) * TILE] = state[tile * RANK : (tile + 1) * RANK, :]


def sweep(parts):
    items = ITEM_TILES * TILE
    return pl.pallas_call(
        sweep_kernel,
        in_specs=[WHOLE] * len(parts),
        out_specs=WHOLE,
        out_shape=jax.ShapeDtypeStruct((RANK, items), jnp.float32),
        scratch_shapes=[
            pltpu.VMEM((ITEM_TILES * RANK, TILE), jnp.float32),
            pltpu.VMEM((ITEM_TILES * RANK, TILE), jnp.float32),
            pltpu.VMEM((RANK, ITEM_TILES, TILE), jnp.float32),
            pltpu.VMEM((GRAM_ROWS, TILE), jnp.float32),
            pltpu.VMEM((GRAM_ROWS, TILE), jnp.float32),
            pltpu.SMEM((GRAM_ROWS, TILE), jnp.float32),
            pltpu.SMEM((GRAM_ROWS, TILE), jnp.float32),
            pltpu.SemaphoreType.DMA((2,)),
        ],
        compiler_params=params(16),
        name="sweep",
    )(*parts)


def shards(tile_values, tile_rows, tile_cols, tile_patterns, tile_counts, factor):
    own = first(factor.T)
    order, starts = plan(tile_rows, tile_cols, tile_counts)
    tiles = prepare(tile_counts, tile_patterns, tile_values)
    parts = []
    for pair in range(PAIRS):
        a, b = own[2 * pair], own[2 * pair + 1]
        a_first, b_first = spread(a), spread(b)
        if pair == 0:
            a_first, b_first, tiles, order, starts = lax.optimization_barrier((a_first, b_first, tiles, order, starts))
        a_line = jnp.concatenate(ring(a_first, 0))
        b_line = jnp.concatenate(ring(b_first, 1))
        a_plane, b_plane = ring(a_line, 1), ring(b_line, 0)
        sums = None
        for part in range(4):
            sums = add_part(part, pair == 0, order, starts, tiles, a_plane[part], b_plane[part], sums)
        parts += [*scatter(pair == 0, sums), a, b]
    return sweep(parts).T


def solution(mesh):
    spec = P(("row", "col"))
    return jax.shard_map(
        shards,
        mesh=mesh,
        in_specs=(P(("row", "col"), None, None), spec, spec, spec, spec, P(("row", "col"), None)),
        out_specs=P(("row", "col"), None),
        check_vma=False,
    )
```

```python
import functools

import jax
import jax.numpy as jnp
from jax import lax
from jax.experimental import pallas as pl
from jax.experimental.pallas import tpu as pltpu
from jax.sharding import PartitionSpec as P

AXES = ("row", "col")
RANK, TILE, SLOTS = 64, 128, 320
HALF_RANK = RANK // 2
GRAM_ROWS = RANK * RANK // TILE
HALF = 8
ITEM_TILES = 16
ROW_TILES = 128
DUMMY = ROW_TILES
UNROLL = 8
BATCH = 32
A_ROWS = (HALF * RANK // 2 + GRAM_ROWS, HALF * RANK // 2)
B_ROWS = (HALF * RANK // 2, HALF * RANK // 2)
CHEAP = pl.CostEstimate(flops=1, bytes_accessed=1, transcendentals=0)

WHOLE = pl.BlockSpec(memory_space=pltpu.VMEM)
SCALARS = pl.BlockSpec(memory_space=pltpu.SMEM)


def params(mib):
    return pltpu.CompilerParams(vmem_limit_bytes=mib * 2**20)


def coords(d):
    return d // 32, (d // 8) % 4, (d // 2) % 4, d % 2


def number(x, y, z, core):
    return ((x * 4 + y) * 4 + z) * 2 + core


def permute(array, move):
    return lax.ppermute(array, AXES, [(d, number(*move(*coords(d)))) for d in range(128)])


def shift(array, axis, step):
    def move(*place):
        return [(p + step) % 4 if i == axis else p for i, p in enumerate(place)]

    return permute(array, move)


def swap_cores(array):
    return permute(array, lambda x, y, z, core: (x, y, z, 1 - core))


def swap(array, axis, across):
    def move(*place):
        return [(3 - p if across else p ^ 1) if i == axis else p for i, p in enumerate(place)]

    return permute(array, move)


def spread(array):
    return permute(array, lambda x, y, z, core: ((x + z + 2 * core) % 4, y if core == 0 else 3 - y, x, y // 2))


def line(head, tail, axis):
    heads = [head, swap(head, axis, False)]
    tails = [tail, swap(tail, axis, True)]
    return [*heads, swap(jnp.concatenate(heads), axis, True), *tails, swap(jnp.concatenate(tails), axis, False)]


def laid_kernel(*refs):
    pieces, out = refs[:-1], refs[-1]
    start = 0
    for piece in pieces:
        out[start : start + piece.shape[0], :] = piece[...]
        start += piece.shape[0]


def laid(pieces, rows):
    return pl.pallas_call(
        laid_kernel,
        in_specs=[WHOLE] * len(pieces),
        out_specs=WHOLE,
        out_shape=jax.ShapeDtypeStruct((4 * sum(rows), TILE), jnp.float32),
        cost_estimate=CHEAP,
        compiler_params=params(6),
        name="laid",
    )(*pieces)


def arranged_kernel(items_ref, *outs):
    for tile in range(HALF // 2, ITEM_TILES):
        start = tile % (HALF // 2) * RANK
        outs[tile // (HALF // 2) - 1][start : start + RANK, :] = items_ref[:, tile * TILE : (tile + 1) * TILE]


def head_kernel(items_ref, out):
    gram = jnp.zeros((RANK, RANK), jnp.float32)
    for tile in range(ITEM_TILES):
        piece = items_ref[:, tile * TILE : (tile + 1) * TILE]
        gram += lax.dot_general(
            piece, piece, (((1,), (1,)), ((), ())), precision=lax.Precision.HIGHEST, preferred_element_type=jnp.float32
        )
        if tile < HALF // 2:
            out[tile * RANK : (tile + 1) * RANK, :] = piece
    out[B_ROWS[0] :, :] = jnp.concatenate([gram[:GRAM_ROWS], gram[GRAM_ROWS:]], axis=1)


def arranged(items):
    def call(kernel, rows, name):
        return pl.pallas_call(
            kernel,
            in_specs=[WHOLE],
            out_specs=[WHOLE] * len(rows),
            out_shape=[jax.ShapeDtypeStruct((n, TILE), jnp.float32) for n in rows],
            cost_estimate=CHEAP,
            compiler_params=params(8),
            name=name,
        )(items)

    return *call(head_kernel, A_ROWS[:1], "head"), *call(arranged_kernel, A_ROWS[1:] + B_ROWS, "arranged")


def split(value):
    high = value.astype(jnp.bfloat16)
    return high, (value - high.astype(jnp.float32)).astype(jnp.bfloat16)


def prepare_kernel(count, patterns, values_ref, tiles_ref):
    step = pl.program_id(0)
    bit = 4 * (lax.broadcasted_iota(jnp.int32, (TILE, TILE), 0) // 32)
    bit += lax.broadcasted_iota(jnp.int32, (TILE, TILE), 1) // 32
    flag = jnp.left_shift(1, bit)

    @pl.when(step * BATCH < count[0])
    def _():
        for u in range(BATCH):
            slot = step * BATCH + u
            kept = jnp.where((patterns[slot] & flag) != 0, values_ref[u], 0.0)
            high, low = split(kept.T)
            tiles_ref[slot, :TILE, :] = high
            tiles_ref[slot, TILE:, :] = low


def prepare(count, patterns, values):
    def block(i, count, patterns):
        return jnp.minimum(i, (count[0] - 1) // BATCH), 0, 0

    return pl.pallas_call(
        prepare_kernel,
        grid_spec=pltpu.PrefetchScalarGridSpec(
            num_scalar_prefetch=2,
            grid=(SLOTS // BATCH,),
            in_specs=[pl.BlockSpec((BATCH, TILE, TILE), block)],
            out_specs=WHOLE,
        ),
        out_shape=pltpu.VMEM((SLOTS, 2 * TILE, TILE), jnp.bfloat16),
        cost_estimate=CHEAP,
        compiler_params=params(10),
        name="prepare",
    )(count, patterns, values)


def plan(rows, cols, count):
    row, col = lax.axis_index("row"), lax.axis_index("col")
    x, y, z, core = row // 4, row % 4, col // 2, col % 2
    shard, tile = cols // ITEM_TILES, cols % ITEM_TILES
    from_z, from_core = (shard % 8) // 2, shard % 2
    from_y = 2 * core + shard // 8
    to_x = (z + from_z + 2 * from_core) % 4
    to_y = jnp.where(from_core == 0, from_y, 3 - from_y)
    def ringed(to, here):
        d = (to - here) % 4
        return jnp.where(d == 0, 0, jnp.where(d == 3, 1, jnp.where(d == 1, 2, 3)))

    def swapped(to, here, second):
        near = to == (here ^ 1)
        across = to == 3 - here
        return jnp.where(to == here, 0, jnp.where(near, 1 + second, jnp.where(across, 2 - second, 3)))

    side, place = tile // HALF, tile % HALF
    second = place // (HALF // 2)
    part = jnp.where(side == 0, ringed(to_y, y), ringed(to_x, x))
    block = jnp.where(side == 0, swapped(to_x, x, second), swapped(to_y, y, second))
    head = jnp.where(side == 0, A_ROWS[0], B_ROWS[0])
    start = jnp.where(second == 0, block * head, 4 * head + block * B_ROWS[1]) + place % (HALF // 2) * RANK
    owner = rows // ITEM_TILES
    target = ((owner % 2 + core) % 2) * 64 + ((owner // 2 - z) % 4) * ITEM_TILES + rows % ITEM_TILES
    slots = jnp.arange(SLOTS, dtype=jnp.int32)
    packed = slots + target * 512 + start // 8 * 131072
    key = part * 2 + side + jnp.where((part == 3) & (target < 64), 2, 0)
    key = jnp.where(slots < count[0], key, 10)
    before = (key[None, :] < key[:, None]) | ((key[None, :] == key[:, None]) & (slots[None, :] < slots[:, None]))
    position = jnp.sum(before.astype(jnp.int32), axis=1)
    places = jnp.arange(SLOTS + 2 * UNROLL, dtype=jnp.int32)
    order = jnp.sum(jnp.where(position[None, :] == places[:, None], packed[None, :], 0), axis=1)
    starts = jnp.sum((key[None, :] < jnp.arange(11, dtype=jnp.int32)[:, None]).astype(jnp.int32), axis=1)
    return order, starts


def products(order, lower, upper, tiles_ref, panel_ref, sums_ref):
    def body(group, carry):
        found = []
        for u in range(UNROLL):
            at = lower + group * UNROLL + u
            word = jnp.where(at < upper, order[at], DUMMY * 512)
            target = (word >> 9) & 255
            high, low = split(panel_ref[pl.ds(pl.multiple_of((word >> 17) * 8, 8), RANK), :])
            both = jnp.concatenate([high, low], axis=0)
            result = jnp.dot(
                jnp.concatenate([both, both], axis=1), tiles_ref[word & 511], preferred_element_type=jnp.float32
            )
            found.append((target, result[:RANK] + result[RANK:]))
        for target, result in found:
            sums_ref[pl.ds(pl.multiple_of(target * RANK, 8), RANK), :] += result
        return carry

    lax.fori_loop(0, (upper - lower + UNROLL - 1) // UNROLL, body, 0)


def part_kernel(keys, fresh, order, starts, tiles_ref, *refs):
    panels, sums_ref = refs[: len(keys)], refs[-1]
    bottom = (ROW_TILES + 1) * RANK
    if fresh:
        sums_ref[...] = jnp.zeros_like(sums_ref)
    for key, panel_ref in zip(keys, panels):
        if key % 2 == 0 and key < 8:
            for block in range(4):
                gram = block * A_ROWS[0] + B_ROWS[0]
                sums_ref[bottom:, :] += panel_ref[gram : gram + GRAM_ROWS, :]
        products(order, starts[key], starts[key + 1], tiles_ref, panel_ref, sums_ref)


def add_parts(order, starts, tiles, parts, sums):
    keys = tuple(sorted(parts))
    operands = [order, starts, tiles] + [parts[key] for key in keys]
    if sums is not None:
        operands.append(sums)
    last = len(operands) - 1
    return pl.pallas_call(
        functools.partial(part_kernel, keys, sums is None),
        in_specs=[SCALARS] * 2 + [WHOLE] * (len(operands) - 2),
        out_specs=WHOLE,
        out_shape=pltpu.VMEM(((ROW_TILES + 1) * RANK + GRAM_ROWS, TILE), jnp.float32),
        input_output_aliases={} if sums is None else {last: 0},
        cost_estimate=CHEAP,
        compiler_params=params(6),
        name="part",
    )(*operands)


def half_of(ref, tile, half):
    return ref[tile * RANK + half * HALF_RANK : tile * RANK + (half + 1) * HALF_RANK, :]


def deal_kernel(sums_ref, *core_refs):
    for half, out in enumerate(core_refs):
        for tile in range(64):
            out[tile * HALF_RANK : (tile + 1) * HALF_RANK, :] = half_of(sums_ref, 64 + tile, half)
    core_refs[0][64 * HALF_RANK :, :] = sums_ref[(ROW_TILES + 1) * RANK :, :]


def deal(sums):
    rows = 64 * HALF_RANK
    return pl.pallas_call(
        deal_kernel,
        in_specs=[WHOLE],
        out_specs=[WHOLE] * 2,
        out_shape=[jax.ShapeDtypeStruct((n, TILE), jnp.float32) for n in (rows + GRAM_ROWS, rows)],
        cost_estimate=CHEAP,
        compiler_params=params(12),
        name="deal",
    )(sums)


def joined_kernel(half, sums_ref, other_ref, *outs):
    size = ITEM_TILES * HALF_RANK
    for place, out in enumerate(outs):
        for tile in range(ITEM_TILES):
            at = place * ITEM_TILES + tile
            rows = slice(tile * HALF_RANK, (tile + 1) * HALF_RANK)
            out[rows, :] = half_of(sums_ref, at, half) + other_ref[at * HALF_RANK : (at + 1) * HALF_RANK, :]
        if half == 0:
            out[size:, :] = sums_ref[(ROW_TILES + 1) * RANK :, :] + other_ref[4 * size :, :]


def joined(half, sums, other):
    rows = ITEM_TILES * HALF_RANK + (GRAM_ROWS if half == 0 else 0)
    return pl.pallas_call(
        functools.partial(joined_kernel, half),
        in_specs=[WHOLE] * 2,
        out_specs=[WHOLE] * 4,
        out_shape=[jax.ShapeDtypeStruct((rows, TILE), jnp.float32)] * 4,
        cost_estimate=CHEAP,
        compiler_params=params(12),
        name="joined",
    )(sums, other)


def onward_kernel(block_ref, passed_ref, out_ref):
    size = ITEM_TILES * HALF_RANK
    out_ref[:size, :] = block_ref[:size, :] + passed_ref[:size, :]
    if out_ref.shape[0] > size:
        out_ref[size:, :] = passed_ref[size:, :]


def onward(block, passed):
    return pl.pallas_call(
        onward_kernel,
        in_specs=[WHOLE] * 2,
        out_specs=WHOLE,
        out_shape=jax.ShapeDtypeStruct(block.shape, jnp.float32),
        cost_estimate=CHEAP,
        compiler_params=params(6),
        name="onward",
    )(block, passed)


def sweep_kernel(*refs):
    factor_ref, blocks = refs[0], refs[1:8]
    out_ref, resid, state, moves, gram_ref, inverse_ref, gram_s, inverse_s, sems = refs[8:]
    size = ITEM_TILES * HALF_RANK
    grams = [ref[size:, :] for ref in blocks[:4]]
    packed = (grams[0] + grams[1]) + (grams[2] + grams[3])
    gram_ref[...] = packed
    inverse_ref[...] = 1.0 / packed
    copies = [
        pltpu.make_async_copy(gram_ref, gram_s, sems.at[0]),
        pltpu.make_async_copy(inverse_ref, inverse_s, sems.at[1]),
    ]
    for copy in copies:
        copy.start()
    gram = jnp.concatenate([packed[:, :RANK], packed[:, RANK:]], axis=0)
    for tile in range(ITEM_TILES):
        rows = slice(tile * HALF_RANK, (tile + 1) * HALF_RANK)
        pieces = [ref[rows, :] for ref in blocks]
        image = jnp.concatenate(
            [pieces[0] + (pieces[2] + pieces[3]), pieces[4] + (pieces[5] + pieces[6])], axis=0
        )
        old = factor_ref[:, tile * TILE : (tile + 1) * TILE]
        fitted = jnp.dot(gram, old, precision=lax.Precision.HIGHEST, preferred_element_type=jnp.float32)
        resid[tile * RANK : (tile + 1) * RANK, :] = image - fitted
        state[tile * RANK : (tile + 1) * RANK, :] = old
    for copy in copies:
        copy.wait()

    def entry(ref, j, k):
        return ref[j % GRAM_ROWS, (j // GRAM_ROWS) * RANK + k]

    def column(ref, k):
        return ref[pl.ds(k, ITEM_TILES, stride=RANK), :]

    for group in range(RANK // 8):
        columns = range(group * 8, group * 8 + 8)
        if group == HALF_RANK // 8:
            for tile in range(ITEM_TILES):
                top, middle, bottom = tile * RANK, tile * RANK + HALF_RANK, (tile + 1) * RANK
                resid[middle:bottom, :] -= jnp.dot(
                    gram[HALF_RANK:, :HALF_RANK],
                    resid[top:middle, :],
                    precision=lax.Precision.HIGHEST,
                    preferred_element_type=jnp.float32,
                )
        left = tuple(column(resid, k) for k in columns)
        for k in range(group * 8 // HALF_RANK * HALF_RANK, group * 8):
            move = moves[k]
            left = tuple(r - move * entry(gram_s, j, k) for r, j in zip(left, columns))
        left = list(left)
        for i, k in enumerate(columns):
            old = column(state, k)
            fresh = jnp.maximum(old + left[i] * entry(inverse_s, k, k), 0.0)
            move = fresh - old
            moves[k] = move
            if k < HALF_RANK:
                resid[pl.ds(k, ITEM_TILES, stride=RANK), :] = move
            state[pl.ds(k, ITEM_TILES, stride=RANK), :] = fresh
            for m in range(i + 1, 8):
                left[m] = left[m] - move * entry(gram_s, columns[m], k)
    for tile in range(ITEM_TILES):
        out_ref[:, tile * TILE : (tile + 1) * TILE] = state[tile * RANK : (tile + 1) * RANK, :]


def sweep(parts):
    items = ITEM_TILES * TILE
    return pl.pallas_call(
        sweep_kernel,
        in_specs=[WHOLE] * len(parts),
        out_specs=WHOLE,
        out_shape=jax.ShapeDtypeStruct((RANK, items), jnp.float32),
        scratch_shapes=[
            pltpu.VMEM((ITEM_TILES * RANK, TILE), jnp.float32),
            pltpu.VMEM((ITEM_TILES * RANK, TILE), jnp.float32),
            pltpu.VMEM((RANK, ITEM_TILES, TILE), jnp.float32),
            pltpu.VMEM((GRAM_ROWS, TILE), jnp.float32),
            pltpu.VMEM((GRAM_ROWS, TILE), jnp.float32),
            pltpu.SMEM((GRAM_ROWS, TILE), jnp.float32),
            pltpu.SMEM((GRAM_ROWS, TILE), jnp.float32),
            pltpu.SemaphoreType.DMA((2,)),
        ],
        compiler_params=params(16),
        name="sweep",
    )(*parts)


def after(value, *others):
    return lax.optimization_barrier((value, others))[0]


def shards(tile_values, tile_rows, tile_cols, tile_patterns, tile_counts, factor):
    items, (order, starts) = lax.optimization_barrier(
        (spread(factor.T), plan(tile_rows, tile_cols, tile_counts))
    )
    a_head, a_tail, b_head, b_tail = arranged(items)
    a_line, b_line = laid(line(a_head, a_tail, 0), A_ROWS), laid(line(b_head, b_tail, 1), B_ROWS)
    tile_values = pltpu.with_memory_space_constraint(tile_values, pltpu.HBM)
    tiles = prepare(tile_counts, after(tile_patterns, a_line, b_line), tile_values)
    add = functools.partial(add_parts, order, starts, tiles)

    a_below, a_above = shift(a_line, 1, 1), shift(a_line, 1, -1)
    b_below, b_above = shift(b_line, 0, 1), shift(b_line, 0, -1)
    sums = add({0: a_line, 1: b_line}, None)
    a_below, a_above, b_below, b_above = (after(block, sums) for block in (a_below, a_above, b_below, b_above))
    cut = a_line.shape[0] // 2
    a_far = jnp.concatenate([shift(a_below[:cut], 1, 1), shift(a_above[cut:], 1, -1)])
    cut = b_line.shape[0] // 2
    b_far = jnp.concatenate([shift(b_below[:cut], 0, 1), shift(b_above[cut:], 0, -1)])
    sums = add({2: a_below, 4: a_above, 3: b_below, 5: b_above}, sums)
    sums = add({7: b_far, 9: b_far}, sums)
    sums = add({6: a_far}, sums)

    messages = deal(sums)
    others = [swap_cores(message) for message in messages]
    sums = add({8: a_far}, after(sums, *messages))
    own, up, across, down = joined(0, sums, others[0])
    sums = after(sums, own)
    passed = shift(across, 2, 1)
    own1, up1, across1, down1 = joined(1, sums, others[1])
    passed1, from_below = shift(across1, 2, -1), shift(up1, 2, 1)
    from_above = shift(after(down, own1), 2, -1)
    found = [own, passed, from_above, shift(onward(up, passed), 2, 1)]
    found += [own1, from_below, shift(onward(down1, passed1), 2, -1)]
    return sweep([factor.T] + found).T


def solution(mesh):
    spec = P(("row", "col"))
    return jax.shard_map(
        shards,
        mesh=mesh,
        in_specs=(P(("row", "col"), None, None), spec, spec, spec, spec, P(("row", "col"), None)),
        out_specs=P(("row", "col"), None),
        check_vma=False,
    )
```

```python
import functools

import jax
import jax.numpy as jnp
from jax import lax
from jax.experimental import pallas as pl
from jax.experimental.pallas import tpu as pltpu
from jax.sharding import PartitionSpec as P

AXES = ("row", "col")
RANK, TILE, SLOTS = 64, 128, 320
HALF_RANK = RANK // 2
GRAM_ROWS = RANK * RANK // TILE
HALF = 8
ITEM_TILES = 16
ROW_TILES = 128
DUMMY = ROW_TILES
UNROLL = 16
BATCH = 32
A_ROWS = (HALF * RANK // 2 + GRAM_ROWS, HALF * RANK // 2)
B_ROWS = (HALF * RANK // 2, HALF * RANK // 2)
CHEAP = pl.CostEstimate(flops=1, bytes_accessed=1, transcendentals=0)

WHOLE = pl.BlockSpec(memory_space=pltpu.VMEM)
SCALARS = pl.BlockSpec(memory_space=pltpu.SMEM)


def params(mib):
    return pltpu.CompilerParams(vmem_limit_bytes=mib * 2**20)


def coords(d):
    return d // 32, (d // 8) % 4, (d // 2) % 4, d % 2


def number(x, y, z, core):
    return ((x * 4 + y) * 4 + z) * 2 + core


def permute(array, move):
    return lax.ppermute(array, AXES, [(d, number(*move(*coords(d)))) for d in range(128)])


def shift(array, axis, step):
    def move(*place):
        return [(p + step) % 4 if i == axis else p for i, p in enumerate(place)]

    return permute(array, move)


def swap_cores(array):
    return permute(array, lambda x, y, z, core: (x, y, z, 1 - core))


def swap(array, axis, across):
    def move(*place):
        return [(3 - p if across else p ^ 1) if i == axis else p for i, p in enumerate(place)]

    return permute(array, move)


def spread(array):
    return permute(array, lambda x, y, z, core: ((x + z + 2 * core) % 4, y if core == 0 else 3 - y, x, y // 2))


def line(head, tail, axis):
    heads = [head, swap(head, axis, False)]
    tails = [tail, swap(tail, axis, True)]
    return [*heads, swap(jnp.concatenate(heads), axis, True), *tails, swap(jnp.concatenate(tails), axis, False)]


def laid_kernel(*refs):
    pieces, out = refs[:-1], refs[-1]
    start = 0
    for piece in pieces:
        out[start : start + piece.shape[0], :] = piece[...]
        start += piece.shape[0]


def laid(pieces, rows):
    return pl.pallas_call(
        laid_kernel,
        in_specs=[WHOLE] * len(pieces),
        out_specs=WHOLE,
        out_shape=jax.ShapeDtypeStruct((4 * sum(rows), TILE), jnp.float32),
        cost_estimate=CHEAP,
        compiler_params=params(6),
        name="laid",
    )(*pieces)


def arranged_kernel(items_ref, *outs):
    for tile in range(HALF // 2, ITEM_TILES):
        start = tile % (HALF // 2) * RANK
        outs[tile // (HALF // 2) - 1][start : start + RANK, :] = items_ref[:, tile * TILE : (tile + 1) * TILE]


def head_kernel(items_ref, out):
    gram = jnp.zeros((RANK, RANK), jnp.float32)
    for tile in range(ITEM_TILES):
        piece = items_ref[:, tile * TILE : (tile + 1) * TILE]
        gram += lax.dot_general(
            piece, piece, (((1,), (1,)), ((), ())), precision=lax.Precision.HIGHEST, preferred_element_type=jnp.float32
        )
        if tile < HALF // 2:
            out[tile * RANK : (tile + 1) * RANK, :] = piece
    out[B_ROWS[0] :, :] = jnp.concatenate([gram[:GRAM_ROWS], gram[GRAM_ROWS:]], axis=1)


def arranged(items):
    def call(kernel, rows, name):
        return pl.pallas_call(
            kernel,
            in_specs=[WHOLE],
            out_specs=[WHOLE] * len(rows),
            out_shape=[jax.ShapeDtypeStruct((n, TILE), jnp.float32) for n in rows],
            cost_estimate=CHEAP,
            compiler_params=params(8),
            name=name,
        )(items)

    return *call(head_kernel, A_ROWS[:1], "head"), *call(arranged_kernel, A_ROWS[1:] + B_ROWS, "arranged")


def split(value):
    high = value.astype(jnp.bfloat16)
    return high, (value - high.astype(jnp.float32)).astype(jnp.bfloat16)


def prepare_kernel(count, patterns, values_ref, tiles_ref):
    step = pl.program_id(0)
    bit = 4 * (lax.broadcasted_iota(jnp.int32, (TILE, TILE), 0) // 32)
    bit += lax.broadcasted_iota(jnp.int32, (TILE, TILE), 1) // 32
    flag = jnp.left_shift(1, bit)

    @pl.when(step * BATCH < count[0])
    def _():
        for u in range(BATCH):
            slot = step * BATCH + u
            kept = jnp.where((patterns[slot] & flag) != 0, values_ref[u], 0.0)
            high, low = split(kept.T)
            tiles_ref[slot, :TILE, :] = high
            tiles_ref[slot, TILE:, :] = low


def prepare(count, patterns, values):
    def block(i, count, patterns):
        return jnp.minimum(i, (count[0] - 1) // BATCH), 0, 0

    return pl.pallas_call(
        prepare_kernel,
        grid_spec=pltpu.PrefetchScalarGridSpec(
            num_scalar_prefetch=2,
            grid=(SLOTS // BATCH,),
            in_specs=[pl.BlockSpec((BATCH, TILE, TILE), block)],
            out_specs=WHOLE,
        ),
        out_shape=pltpu.VMEM((SLOTS, 2 * TILE, TILE), jnp.bfloat16),
        cost_estimate=CHEAP,
        compiler_params=params(10),
        name="prepare",
    )(count, patterns, values)


def plan(rows, cols, count):
    row, col = lax.axis_index("row"), lax.axis_index("col")
    x, y, z, core = row // 4, row % 4, col // 2, col % 2
    shard, tile = cols // ITEM_TILES, cols % ITEM_TILES
    from_z, from_core = (shard % 8) // 2, shard % 2
    from_y = 2 * core + shard // 8
    to_x = (z + from_z + 2 * from_core) % 4
    to_y = jnp.where(from_core == 0, from_y, 3 - from_y)
    def ringed(to, here):
        d = (to - here) % 4
        return jnp.where(d == 0, 0, jnp.where(d == 3, 1, jnp.where(d == 1, 2, 3)))

    def swapped(to, here, second):
        near = to == (here ^ 1)
        across = to == 3 - here
        return jnp.where(to == here, 0, jnp.where(near, 1 + second, jnp.where(across, 2 - second, 3)))

    side, place = tile // HALF, tile % HALF
    second = place // (HALF // 2)
    part = jnp.where(side == 0, ringed(to_y, y), ringed(to_x, x))
    block = jnp.where(side == 0, swapped(to_x, x, second), swapped(to_y, y, second))
    head = jnp.where(side == 0, A_ROWS[0], B_ROWS[0])
    start = jnp.where(second == 0, block * head, 4 * head + block * B_ROWS[1]) + place % (HALF // 2) * RANK
    owner = rows // ITEM_TILES
    target = ((owner % 2 + core) % 2) * 64 + ((owner // 2 - z) % 4) * ITEM_TILES + rows % ITEM_TILES
    slots = jnp.arange(SLOTS, dtype=jnp.int32)
    packed = slots + target * 512 + start // 8 * 131072
    key = part * 2 + side + jnp.where((part == 3) & (target < 64), 2, 0)
    key = jnp.where(slots < count[0], key, 10)
    before = (key[None, :] < key[:, None]) | ((key[None, :] == key[:, None]) & (slots[None, :] < slots[:, None]))
    position = jnp.sum(before.astype(jnp.int32), axis=1)
    places = jnp.arange(SLOTS + 2 * UNROLL, dtype=jnp.int32)
    order = jnp.sum(jnp.where(position[None, :] == places[:, None], packed[None, :], 0), axis=1)
    starts = jnp.sum((key[None, :] < jnp.arange(11, dtype=jnp.int32)[:, None]).astype(jnp.int32), axis=1)
    return order, starts


def products(order, lower, upper, tiles_ref, panel_ref, sums_ref):
    def body(group, carry):
        found = []
        for u in range(UNROLL):
            at = lower + group * UNROLL + u
            word = jnp.where(at < upper, order[at], DUMMY * 512)
            target = (word >> 9) & 255
            high, low = split(panel_ref[pl.ds(pl.multiple_of((word >> 17) * 8, 8), RANK), :])
            both = jnp.concatenate([high, low], axis=0)
            result = jnp.dot(
                jnp.concatenate([both, both], axis=1), tiles_ref[word & 511], preferred_element_type=jnp.float32
            )
            found.append((target, result[:RANK] + result[RANK:]))
        for target, result in found:
            sums_ref[pl.ds(pl.multiple_of(target * RANK, 8), RANK), :] += result
        return carry

    lax.fori_loop(0, (upper - lower + UNROLL - 1) // UNROLL, body, 0)


def part_kernel(keys, fresh, order, starts, tiles_ref, *refs):
    panels, sums_ref = refs[: len(keys)], refs[-1]
    bottom = (ROW_TILES + 1) * RANK
    if fresh:
        sums_ref[...] = jnp.zeros_like(sums_ref)
    for key, panel_ref in zip(keys, panels):
        if key % 2 == 0 and key < 8:
            for block in range(4):
                gram = block * A_ROWS[0] + B_ROWS[0]
                sums_ref[bottom:, :] += panel_ref[gram : gram + GRAM_ROWS, :]
        products(order, starts[key], starts[key + 1], tiles_ref, panel_ref, sums_ref)


def add_parts(order, starts, tiles, parts, sums):
    keys = tuple(sorted(parts))
    operands = [order, starts, tiles] + [parts[key] for key in keys]
    if sums is not None:
        operands.append(sums)
    last = len(operands) - 1
    return pl.pallas_call(
        functools.partial(part_kernel, keys, sums is None),
        in_specs=[SCALARS] * 2 + [WHOLE] * (len(operands) - 2),
        out_specs=WHOLE,
        out_shape=pltpu.VMEM(((ROW_TILES + 1) * RANK + GRAM_ROWS, TILE), jnp.float32),
        input_output_aliases={} if sums is None else {last: 0},
        cost_estimate=CHEAP,
        compiler_params=params(6),
        name="part",
    )(*operands)


def half_of(ref, tile, half):
    return ref[tile * RANK + half * HALF_RANK : tile * RANK + (half + 1) * HALF_RANK, :]


def deal_kernel(sums_ref, *core_refs):
    for half, out in enumerate(core_refs):
        for tile in range(64):
            out[tile * HALF_RANK : (tile + 1) * HALF_RANK, :] = half_of(sums_ref, 64 + tile, half)
    core_refs[0][64 * HALF_RANK :, :] = sums_ref[(ROW_TILES + 1) * RANK :, :]


def deal(sums):
    rows = 64 * HALF_RANK
    return pl.pallas_call(
        deal_kernel,
        in_specs=[WHOLE],
        out_specs=[WHOLE] * 2,
        out_shape=[jax.ShapeDtypeStruct((n, TILE), jnp.float32) for n in (rows + GRAM_ROWS, rows)],
        cost_estimate=CHEAP,
        compiler_params=params(12),
        name="deal",
    )(sums)


def joined_kernel(half, sums_ref, other_ref, *outs):
    size = ITEM_TILES * HALF_RANK
    for place, out in enumerate(outs):
        for tile in range(ITEM_TILES):
            at = place * ITEM_TILES + tile
            rows = slice(tile * HALF_RANK, (tile + 1) * HALF_RANK)
            out[rows, :] = half_of(sums_ref, at, half) + other_ref[at * HALF_RANK : (at + 1) * HALF_RANK, :]
        if half == 0:
            out[size:, :] = sums_ref[(ROW_TILES + 1) * RANK :, :] + other_ref[4 * size :, :]


def joined(half, sums, other):
    rows = ITEM_TILES * HALF_RANK + (GRAM_ROWS if half == 0 else 0)
    return pl.pallas_call(
        functools.partial(joined_kernel, half),
        in_specs=[WHOLE] * 2,
        out_specs=[WHOLE] * 4,
        out_shape=[jax.ShapeDtypeStruct((rows, TILE), jnp.float32)] * 4,
        cost_estimate=CHEAP,
        compiler_params=params(12),
        name="joined",
    )(sums, other)


def onward_kernel(block_ref, passed_ref, out_ref):
    size = ITEM_TILES * HALF_RANK
    out_ref[:size, :] = block_ref[:size, :] + passed_ref[:size, :]
    if out_ref.shape[0] > size:
        out_ref[size:, :] = passed_ref[size:, :]


def onward(block, passed):
    return pl.pallas_call(
        onward_kernel,
        in_specs=[WHOLE] * 2,
        out_specs=WHOLE,
        out_shape=jax.ShapeDtypeStruct(block.shape, jnp.float32),
        cost_estimate=CHEAP,
        compiler_params=params(6),
        name="onward",
    )(block, passed)


def sweep_kernel(*refs):
    factor_ref, blocks = refs[0], refs[1:8]
    out_ref, resid, state, moves, gram_ref, inverse_ref, gram_s, inverse_s, sems = refs[8:]
    size = ITEM_TILES * HALF_RANK
    grams = [ref[size:, :] for ref in blocks[:4]]
    packed = (grams[0] + grams[1]) + (grams[2] + grams[3])
    gram_ref[...] = packed
    inverse_ref[...] = 1.0 / packed
    copies = [
        pltpu.make_async_copy(gram_ref, gram_s, sems.at[0]),
        pltpu.make_async_copy(inverse_ref, inverse_s, sems.at[1]),
    ]
    for copy in copies:
        copy.start()
    gram = jnp.concatenate([packed[:, :RANK], packed[:, RANK:]], axis=0)
    for tile in range(ITEM_TILES):
        rows = slice(tile * HALF_RANK, (tile + 1) * HALF_RANK)
        pieces = [ref[rows, :] for ref in blocks]
        image = jnp.concatenate(
            [pieces[0] + (pieces[2] + pieces[3]), pieces[4] + (pieces[5] + pieces[6])], axis=0
        )
        old = factor_ref[:, tile * TILE : (tile + 1) * TILE]
        fitted = jnp.dot(gram, old, precision=lax.Precision.HIGHEST, preferred_element_type=jnp.float32)
        resid[tile * RANK : (tile + 1) * RANK, :] = image - fitted
        state[tile * RANK : (tile + 1) * RANK, :] = old
    for copy in copies:
        copy.wait()

    def entry(ref, j, k):
        return ref[j % GRAM_ROWS, (j // GRAM_ROWS) * RANK + k]

    def column(ref, k):
        return ref[pl.ds(k, ITEM_TILES, stride=RANK), :]

    for group in range(RANK // 8):
        columns = range(group * 8, group * 8 + 8)
        if group == HALF_RANK // 8:
            for tile in range(ITEM_TILES):
                top, middle, bottom = tile * RANK, tile * RANK + HALF_RANK, (tile + 1) * RANK
                resid[middle:bottom, :] -= jnp.dot(
                    gram[HALF_RANK:, :HALF_RANK],
                    resid[top:middle, :],
                    precision=lax.Precision.HIGHEST,
                    preferred_element_type=jnp.float32,
                )
        left = tuple(column(resid, k) for k in columns)
        for k in range(group * 8 // HALF_RANK * HALF_RANK, group * 8):
            move = moves[k]
            left = tuple(r - move * entry(gram_s, j, k) for r, j in zip(left, columns))
        left = list(left)
        for i, k in enumerate(columns):
            old = column(state, k)
            fresh = jnp.maximum(old + left[i] * entry(inverse_s, k, k), 0.0)
            move = fresh - old
            moves[k] = move
            if k < HALF_RANK:
                resid[pl.ds(k, ITEM_TILES, stride=RANK), :] = move
            state[pl.ds(k, ITEM_TILES, stride=RANK), :] = fresh
            for m in range(i + 1, 8):
                left[m] = left[m] - move * entry(gram_s, columns[m], k)
    for tile in range(ITEM_TILES):
        out_ref[:, tile * TILE : (tile + 1) * TILE] = state[tile * RANK : (tile + 1) * RANK, :]


def sweep(parts):
    items = ITEM_TILES * TILE
    return pl.pallas_call(
        sweep_kernel,
        in_specs=[WHOLE] * len(parts),
        out_specs=WHOLE,
        out_shape=jax.ShapeDtypeStruct((RANK, items), jnp.float32),
        scratch_shapes=[
            pltpu.VMEM((ITEM_TILES * RANK, TILE), jnp.float32),
            pltpu.VMEM((ITEM_TILES * RANK, TILE), jnp.float32),
            pltpu.VMEM((RANK, ITEM_TILES, TILE), jnp.float32),
            pltpu.VMEM((GRAM_ROWS, TILE), jnp.float32),
            pltpu.VMEM((GRAM_ROWS, TILE), jnp.float32),
            pltpu.SMEM((GRAM_ROWS, TILE), jnp.float32),
            pltpu.SMEM((GRAM_ROWS, TILE), jnp.float32),
            pltpu.SemaphoreType.DMA((2,)),
        ],
        compiler_params=params(16),
        name="sweep",
    )(*parts)


def after(value, *others):
    return lax.optimization_barrier((value, others))[0]


def shards(tile_values, tile_rows, tile_cols, tile_patterns, tile_counts, factor):
    items, (order, starts) = lax.optimization_barrier(
        (spread(factor.T), plan(tile_rows, tile_cols, tile_counts))
    )
    a_head, a_tail, b_head, b_tail = arranged(items)
    a_line, b_line = laid(line(a_head, a_tail, 0), A_ROWS), laid(line(b_head, b_tail, 1), B_ROWS)
    tile_values = pltpu.with_memory_space_constraint(tile_values, pltpu.HBM)
    tiles = prepare(tile_counts, after(tile_patterns, a_line, b_line), tile_values)
    add = functools.partial(add_parts, order, starts, tiles)

    a_below, a_above = shift(a_line, 1, 1), shift(a_line, 1, -1)
    b_below, b_above = shift(b_line, 0, 1), shift(b_line, 0, -1)
    sums = add({0: a_line, 1: b_line}, None)
    a_below, a_above, b_below, b_above = (after(block, sums) for block in (a_below, a_above, b_below, b_above))
    cut = a_line.shape[0] // 2
    a_far = jnp.concatenate([shift(a_below[:cut], 1, 1), shift(a_above[cut:], 1, -1)])
    cut = b_line.shape[0] // 2
    b_far = jnp.concatenate([shift(b_below[:cut], 0, 1), shift(b_above[cut:], 0, -1)])
    sums = add({2: a_below, 4: a_above, 3: b_below, 5: b_above}, sums)
    sums = add({7: b_far, 9: b_far}, sums)
    sums = add({6: a_far}, sums)

    messages = deal(sums)
    others = [swap_cores(message) for message in messages]
    sums = add({8: a_far}, after(sums, *messages))
    own, up, across, down = joined(0, sums, others[0])
    sums = after(sums, own)
    passed = shift(across, 2, 1)
    own1, up1, across1, down1 = joined(1, sums, others[1])
    passed1, from_below = shift(across1, 2, -1), shift(up1, 2, 1)
    from_above = shift(after(down, own1), 2, -1)
    found = [own, passed, from_above, shift(onward(up, passed), 2, 1)]
    found += [own1, from_below, shift(onward(down1, passed1), 2, -1)]
    return sweep([factor.T] + found).T


def solution(mesh):
    spec = P(("row", "col"))
    return jax.shard_map(
        shards,
        mesh=mesh,
        in_specs=(P(("row", "col"), None, None), spec, spec, spec, spec, P(("row", "col"), None)),
        out_specs=P(("row", "col"), None),
        check_vma=False,
    )
```
